256 devices in a mesh: dp: 8 (over x_hi, y), tp: 32 (over x_lo, z, core).
Axes of the slice: x: 4 (x_hi: 2, x_lo: 2; x = x_hi * 2 + x_lo), y: 4, z: 8, core: 2. Of those that a mesh axis runs over, the one named last changes fastest.
Arguments:
- moe_input: bfloat16 [1024, 7168], P(('dp', 'tp')), may hold values from -6 to 6
- route_ids: int32 [1024, 8], P(('dp', 'tp')), may hold values from 0 to 31, all different within a row; in each aligned block of 4 rows (0 to 3, 4 to 7, ...) at most 2 rows name the same one
- route_weight: bfloat16 [1024, 8], P(('dp', 'tp')), may hold values from 0.099609375 to 1
- gate_weight: bfloat16 [32, 7168, 1024], P('tp', None, 'dp'), may hold values from -0.0625 to 0.0625
- up_weight: bfloat16 [32, 7168, 1024], P('tp', None, 'dp'), may hold values from -0.0625 to 0.0625
- down_weight: bfloat16 [32, 1024, 7168], P('tp', 'dp'), may hold values from -0.1875 to 0.1875
- att_query: bfloat16 [1024, 128, 576], P(('dp', 'tp')), may hold values from -8 to 8
- att_cache: bfloat16 [1024, 512, 576], P(('dp', 'tp')), may hold values from -6 to 6
- cache_length: int32 [1024], P(('dp', 'tp')), may hold values from 2 to 512, as said below
Outputs:
- moe_output: bfloat16 [1024, 7168], P(('dp', 'tp'))
- context: bfloat16 [1024, 128, 512], P(('dp', 'tp'))
The draws below stay inside these ranges and needn't reach their ends.
Inputs may be any that keep to these rules, and one draw needn't show every extreme that they name: `route_ids`: each row names 8 different experts. Within the rows of one device (aligned blocks of 4 rows) no expert is named by more than 2 rows, and in every draw some expert is named by exactly 2 rows of some device. `cache_length`: the first row of every aligned block of 4 rows has all 512 positions filled.
All inputs are finite; a program needn't handle non-finite values.
Results may differ from the reference program's by a relative error of at most 0.0055.
Values may be sent and summed in bfloat16 or wider, within the bound.
No kernel may reach another device: no remote copies, remote signals or barrier semaphores. Data moves between devices by JAX's collectives and lax.ppermute only.
A program may use at most 128 MiB of HBM per device.

```python
import math
import jax
import jax.numpy as jnp
import numpy as np
from jax import lax

D = 7168
HEADS = 128
LATENT = 512
ROPE = 64
TOP = 8
FF = 1024
ROWS_DEV = 4
CACHE = 512
EXPERTS = 32
CAP = 2
TOKENS = 1024
DEVICES = 256


def draw_att_query(key, part):
    key = jax.random.fold_in(key, 21)
    queries = jnp.clip(jax.random.normal(key, (TOKENS, HEADS, LATENT + ROPE), jnp.float32), -8.0, 8.0)
    return queries.astype(jnp.bfloat16)


def draw_att_cache(key, part):
    key = jax.random.fold_in(key, 22)
    latents = jnp.clip(jax.random.normal(key, (TOKENS, CACHE, LATENT + ROPE), jnp.float32), -6.0, 6.0)
    return latents.astype(jnp.bfloat16)


def draw_cache_length(key, part):
    key = jax.random.fold_in(key, 23)
    lengths = jax.random.randint(key, (TOKENS,), 2, CACHE + 1, dtype=jnp.int32)
    leading = jnp.arange(TOKENS) % ROWS_DEV == 0
    return jnp.where(leading, CACHE, lengths).astype(jnp.int32)


def block_scale(own_key, extent, split, smallest, top_value):
    gain, own = 1.0, jax.random.fold_in(own_key, 6)
    for dim, blocks in split:
        steps = jnp.exp(jax.random.uniform(jax.random.fold_in(own, dim), (blocks,), jnp.float32, smallest / len(split), top_value / len(split)))
        gain = gain * jnp.repeat(steps, extent[dim] // blocks).reshape([-1 if axis == dim else 1 for axis in range(len(extent))])
    return gain


def assign_block(rng, own, number, rows, amount, top, bound, skew):
    order = jax.random.permutation(rng, amount)
    crowded, usual = portions_of(amount, rows * top, bound, skew, True), portions_of(amount, rows * top, bound, skew, False)
    places = jnp.arange(amount)

    def named(tallies, turn):
        used = int((tallies > 0).sum())
        fixed = max(1, used // 4)
        moved = fixed + (places - fixed + turn * (used - fixed)) % max(1, amount - fixed)
        return jnp.zeros((amount,), jnp.int32).at[order[jnp.where(places < fixed, places, moved)]].set(jnp.asarray(tallies, jnp.int32))

    tallies = jnp.where(number % 4 == 0, named(crowded, number // 4), named(usual, number - number // 4 - 1))
    mixed = jax.random.permutation(jax.random.fold_in(own, 3), amount)
    donor, taker = mixed[0:amount // 2 * 2:2], mixed[1:amount // 2 * 2:2]
    margin = jnp.minimum(tallies[donor] - 1, bound - tallies[taker]) // 2
    margin = jnp.where((donor == order[0]) | (taker == order[0]) | (tallies[taker] == 0), 0, jnp.maximum(margin, 0))
    moved = jax.random.randint(jax.random.fold_in(own, 4), (amount // 2,), 0, 1 << 20) % (margin + 1)
    tallies = tallies.at[donor].add(-moved).at[taker].add(moved)
    members = jnp.searchsorted(jnp.cumsum(tallies), jnp.arange(rows * top), side="right").astype(jnp.int32)
    grid = members.reshape(top, rows).T
    grid = grid[jax.random.permutation(jax.random.fold_in(own, 1), rows)]
    turn = jax.random.randint(jax.random.fold_in(own, 2), (rows, 1), 0, top)
    return jnp.take_along_axis(grid, (jnp.arange(top)[None, :] + turn) % top, axis=1)


def portions_of(count, total, most, skew, full):
    weights = [(1 << 20) // math.isqrt(standing ** skew) + 1 for standing in range(1, count + 1)]
    largest = most if full else min(most, max(-(-total // count), total * weights[0] // sum(weights)))
    least = 1 if total - largest >= count - 1 else 0
    given, surplus = [largest] + [least] * (count - 1), total - largest - least * (count - 1)
    while surplus > 0:
        movable = [i for i in range(1, count) if given[i] < largest] or [i for i in range(1, count) if given[i] < most]
        mass, left = sum([weights[i] for i in movable]), surplus
        for i in movable:
            more = min(most - given[i], max(1, left * weights[i] // mass), surplus)
            given[i] = given[i] + more
            surplus = surplus - more
    return np.array(given)


def gaussian(rng, extent, deviation, reach, pieces=(), kind=jnp.bfloat16):
    loudness = block_scale(rng, extent, pieces, -0.22, 0.18) if pieces else 1.0
    result = jax.random.normal(rng, extent, jnp.float32) * deviation * loudness
    return jnp.minimum(jnp.maximum(result, -reach), reach).astype(kind)


def setup_inputs(seed: int = 0) -> dict:
    seeds = jax.random.split(jax.random.key(seed), 10)
    moe_input = gaussian(seeds[0], (TOKENS, D), 1.0, 6.0, ((0, 256),))
    route_ids_keys = jax.random.split(jax.random.fold_in(seeds[1], 1), TOKENS // ROWS_DEV)
    route_ids_turns = jax.random.permutation(jax.random.fold_in(seeds[1], 3), TOKENS // ROWS_DEV)
    route_ids = jax.vmap(lambda own, number: assign_block(jax.random.fold_in(seeds[1], 2), own, number, ROWS_DEV, EXPERTS, TOP, CAP, 1))(route_ids_keys, route_ids_turns).reshape((TOKENS, TOP))
    route_weight = jnp.clip(0.099609375 + 0.9003906 * jax.random.uniform(seeds[2], (TOKENS, TOP), jnp.float32) ** block_scale(seeds[2], (TOKENS, TOP), ((0, 256),), -0.2, 0.2), 0.099609375, 1.0).astype(jnp.bfloat16)
    gate_weight = gaussian(seeds[3], (EXPERTS, D, FF), D ** -0.5, 0.0625, ((0, 32), (2, 8)))
    up_weight = gaussian(seeds[4], (EXPERTS, D, FF), D ** -0.5, 0.0625, ((0, 32), (2, 8)))
    down_weight = gaussian(seeds[5], (EXPERTS, FF, D), FF ** -0.5, 0.1875, ((0, 32), (1, 8)))
    att_query = draw_att_query(jax.random.fold_in(seeds[9], 71), 0)
    att_cache = draw_att_cache(jax.random.fold_in(seeds[9], 71), 0)
    cache_length = draw_cache_length(jax.random.fold_in(seeds[9], 71), 0)
    return dict(moe_input=moe_input, route_ids=route_ids, route_weight=route_weight, gate_weight=gate_weight, up_weight=up_weight, down_weight=down_weight, att_query=att_query, att_cache=att_cache, cache_length=cache_length)


softmax_scale = 192.0 ** -0.5


def expert_block(moe_input, route_ids, route_weight, gate_weight, up_weight, down_weight):
    blocks = TOKENS // ROWS_DEV
    one_hot = (route_ids[:, :, None] == jnp.arange(EXPERTS, dtype=jnp.int32)[None, None, :]).astype(jnp.int32)
    per_row = jnp.sum(one_hot, axis=1).reshape(blocks, ROWS_DEV, EXPERTS)
    before = (jnp.cumsum(per_row, axis=1) - per_row).reshape(TOKENS, EXPERTS)
    slot_of = jnp.sum(one_hot * before[:, None, :], axis=2).astype(jnp.int32)
    row_index = jnp.arange(TOKENS, dtype=jnp.int32)
    positions = ((row_index // ROWS_DEV)[:, None] * CAP + slot_of).astype(jnp.int32)
    padded = jnp.concatenate([moe_input, jnp.zeros((1, D), moe_input.dtype)], axis=0)
    every_row = jnp.broadcast_to(row_index[:, None], (TOKENS, TOP)).reshape(-1)
    weights_all = route_weight.astype(jnp.float32)

    def one_expert(running, expert_id):
        routed = route_ids == expert_id
        where_to = jnp.where(routed, positions, DEVICES * CAP).reshape(-1).astype(jnp.int32)
        chosen_rows = jnp.full((DEVICES * CAP,), TOKENS, jnp.int32).at[where_to].set(every_row, mode="drop")
        chosen = padded[chosen_rows]
        gate_act = jnp.dot(chosen, gate_weight[expert_id], preferred_element_type=jnp.float32)
        up_act = jnp.dot(chosen, up_weight[expert_id], preferred_element_type=jnp.float32)
        hidden = (jax.nn.silu(gate_act) * up_act).astype(jnp.bfloat16)
        outputs = jnp.dot(hidden, down_weight[expert_id], preferred_element_type=jnp.float32)
        weight = jnp.sum(jnp.where(routed, weights_all, jnp.zeros_like(weights_all)), axis=1)
        position = jnp.sum(jnp.where(routed, positions, 0), axis=1).astype(jnp.int32)
        return running + weight[:, None] * outputs[position], None

    start = jnp.zeros((TOKENS, D), jnp.float32)
    totals, _ = lax.scan(one_expert, start, jnp.arange(EXPERTS, dtype=jnp.int32))
    return totals.astype(jnp.bfloat16)


def attend_block(inputs):
    queries, latents, length = inputs
    query_wide = queries.astype(jnp.float32)
    latent_wide = latents.astype(jnp.float32)
    scores = jnp.einsum("rhc,rlc->rhl", query_wide, latent_wide) * softmax_scale
    visible = jnp.arange(CACHE, dtype=jnp.int32)[None, None, :] < length[:, None, None]
    scores = jnp.where(visible, scores, -jnp.inf)
    highest = jnp.max(scores, axis=-1, keepdims=True)
    weight = jnp.exp(scores - highest)
    probs = (weight / jnp.sum(weight, axis=-1, keepdims=True)).astype(jnp.bfloat16)
    values = latents[:, :, :LATENT].astype(jnp.float32)
    context = jnp.einsum("rhl,rlc->rhc", probs.astype(jnp.float32), values)
    return context.astype(jnp.bfloat16)


def reference(moe_input, route_ids, route_weight, gate_weight, up_weight, down_weight, att_query, att_cache, cache_length):
    moe_output = expert_block(moe_input, route_ids, route_weight, gate_weight, up_weight, down_weight)
    blocks = TOKENS // ROWS_DEV
    grouped = (att_query.reshape(blocks, ROWS_DEV, HEADS, LATENT + ROPE),
               att_cache.reshape(blocks, ROWS_DEV, CACHE, LATENT + ROPE),
               cache_length.reshape(blocks, ROWS_DEV))
    context = lax.map(attend_block, grouped).reshape(TOKENS, HEADS, LATENT)
    return (moe_output, context)
```

```python
import jax
import jax.numpy as jnp
from jax import lax
from jax.sharding import Mesh, PartitionSpec as P

LATENT = 512
AXES = ("xh", "y", "xl", "z", "core")
SIZES = (2, 4, 2, 8, 2)
LENGTH = {"x": 4, "y": 4, "z": 8}
NAMES = {"x": ("xh", "xl"), "y": "y", "z": "z"}
softmax_scale = 192.0 ** (-0.5)


def shift(value, axis, by):
    n = LENGTH[axis]
    return lax.ppermute(value, NAMES[axis], [(i, (i + by) % n) for i in range(n)])


def attend(queries, latents, length):
    scores = (
        jnp.einsum("rhc,rlc->rhl", queries, latents, preferred_element_type=jnp.float32)
        * softmax_scale
    )
    visible = jnp.arange(latents.shape[1], dtype=jnp.int32)[None, None, :] < length[:, None, None]
    scores = jnp.where(visible, scores, -jnp.inf)
    highest = jnp.max(scores, axis=-1, keepdims=True)
    weight = jnp.exp(scores - highest)
    probs = (weight / jnp.sum(weight, axis=-1, keepdims=True)).astype(jnp.bfloat16)
    context = jnp.einsum(
        "rhl,rlc->rhc", probs, latents[:, :, :LATENT], preferred_element_type=jnp.float32
    )
    return context.astype(jnp.bfloat16)


def gather_direct(value, axis, dim):
    n = LENGTH[axis]
    return jnp.concatenate([value] + [shift(value, axis, k) for k in range(1, n)], axis=dim)


def gather_ring4(value, axis, dim, half_dim):
    half = value.shape[half_dim] // 2
    below = shift(value, axis, 1)
    above = shift(value, axis, -1)
    low = lax.slice_in_dim(below, 0, half, axis=half_dim)
    high = lax.slice_in_dim(above, half, 2 * half, axis=half_dim)
    opposite = jnp.concatenate([shift(low, axis, 1), shift(high, axis, -1)], axis=half_dim)
    return jnp.concatenate([value, below, opposite, above], axis=dim)


def wide(value):
    return value.astype(jnp.float32)


def narrow(value):
    return value.astype(jnp.bfloat16)


def scatter_direct(value, axis, dim):
    n = LENGTH[axis]
    parts = jnp.split(value, n, axis=dim)
    total = wide(parts[0])
    for k in range(1, n):
        total = total + wide(shift(parts[k], axis, -k))
    return narrow(total)


def scatter_ring4(value, axis, dim, half_dim):
    own, below, opposite, above = jnp.split(value, 4, axis=dim)
    half = own.shape[half_dim] // 2
    low = lax.slice_in_dim(opposite, 0, half, axis=half_dim)
    high = lax.slice_in_dim(opposite, half, 2 * half, axis=half_dim)
    low = shift(low, axis, -1)
    high = shift(high, axis, 1)
    below_low = lax.slice_in_dim(below, 0, half, axis=half_dim)
    below_high = lax.slice_in_dim(below, half, 2 * half, axis=half_dim)
    above_low = lax.slice_in_dim(above, 0, half, axis=half_dim)
    above_high = lax.slice_in_dim(above, half, 2 * half, axis=half_dim)
    below = jnp.concatenate([narrow(wide(below_low) + wide(low)), below_high], axis=half_dim)
    above = jnp.concatenate([above_low, narrow(wide(above_high) + wide(high))], axis=half_dim)
    return narrow(wide(own) + wide(shift(below, axis, -1)) + wide(shift(above, axis, 1)))


def on_device(
    moe_input,
    route_ids,
    route_weight,
    gate_weight,
    up_weight,
    down_weight,
    att_query,
    att_cache,
    cache_length,
):
    rows, width = moe_input.shape
    routes = route_ids.shape[1]
    half = width // 2
    swap = [(0, 1), (1, 0)]
    w_own = jnp.concatenate([gate_weight[0], up_weight[0]], axis=1)
    d_own = down_weight[0]
    w_other = lax.ppermute(w_own, "core", swap)
    d_other = lax.ppermute(d_own, "core", swap)
    context = attend(att_query, att_cache, cache_length)

    tail = jnp.zeros((rows, 128 - 2 * routes), jnp.bfloat16)
    sent = jnp.concatenate([moe_input, route_ids.astype(jnp.bfloat16), route_weight, tail], axis=1)
    sent = gather_direct(sent[None], "z", 0).reshape(1, 1, 8 * rows, width + 128)
    first, second = sent[..., :half], sent[..., half:]
    first = gather_ring4(gather_direct(first, "x", 0), "y", 1, 0)
    second = gather_ring4(gather_direct(second, "y", 1), "x", 0, 1)
    first = first.reshape(-1, half)
    second = second.reshape(-1, half + 128)
    ids = second[:, half : half + routes].astype(jnp.int32)
    weights = wide(second[:, half + routes : half + 2 * routes])
    second = second[:, :half]

    me = lax.axis_index(("xl", "z", "core"))

    def hidden_of(expert, w):
        act = jnp.dot(first, w[:half], preferred_element_type=jnp.float32)
        act = act + jnp.dot(second, w[half:], preferred_element_type=jnp.float32)
        units = act.shape[1] // 2
        hidden = jax.nn.silu(act[:, :units]) * act[:, units:]
        weight = jnp.sum(jnp.where(ids == expert, weights, 0.0), axis=1, keepdims=True)
        return narrow(hidden * weight)

    hidden = jnp.concatenate([hidden_of(me, w_own), hidden_of(me ^ 1, w_other)], axis=1)
    down = jnp.concatenate([d_own, d_other], axis=0)
    first = narrow(jnp.dot(hidden, down[:, :half], preferred_element_type=jnp.float32))
    second = narrow(jnp.dot(hidden, down[:, half:], preferred_element_type=jnp.float32))
    first = first.reshape(4, 4, 8 * rows, half)
    second = second.reshape(4, 4, 8 * rows, half)
    first = scatter_direct(scatter_ring4(first, "y", 1, 0), "x", 0)
    second = scatter_direct(scatter_ring4(second, "x", 0, 1), "y", 1)
    mixed = jnp.concatenate([first, second], axis=-1).reshape(8, rows, width)
    return scatter_direct(mixed, "z", 0)[0], context


def solution(mesh):
    fine = Mesh(mesh.devices.reshape(SIZES), AXES)
    every = AXES
    tp = ("xl", "z", "core")
    dp = ("xh", "y")
    in_specs = (
        P(every, None),
        P(every, None),
        P(every, None),
        P(tp, None, dp),
        P(tp, None, dp),
        P(tp, dp, None),
        P(every, None, None),
        P(every, None, None),
        P(every),
    )
    out_specs = (P(every, None), P(every, None, None))
    return jax.shard_map(
        on_device, mesh=fine, in_specs=in_specs, out_specs=out_specs, check_vma=False
    )
```

```python
import jax
import jax.numpy as jnp
from jax import lax
from jax.experimental import pallas as pl
from jax.experimental.pallas import tpu as pltpu
from jax.sharding import Mesh, PartitionSpec as P

LATENT = 512
AXES = ("xh", "y", "xl", "z", "core")
SIZES = (2, 4, 2, 8, 2)
LENGTH = {"x": 4, "y": 4, "z": 8}
NAMES = {"x": ("xh", "xl"), "y": "y", "z": "z"}
softmax_scale = 192.0 ** (-0.5)


def shift(value, axis, by):
    n = LENGTH[axis]
    return lax.ppermute(value, NAMES[axis], [(i, (i + by) % n) for i in range(n)])


def attend(queries, latents, length):
    scores = (
        jnp.einsum("rhc,rlc->rhl", queries, latents, preferred_element_type=jnp.float32)
        * softmax_scale
    )
    visible = jnp.arange(latents.shape[1], dtype=jnp.int32)[None, None, :] < length[:, None, None]
    scores = jnp.where(visible, scores, -jnp.inf)
    highest = jnp.max(scores, axis=-1, keepdims=True)
    weight = jnp.exp(scores - highest)
    probs = (weight / jnp.sum(weight, axis=-1, keepdims=True)).astype(jnp.bfloat16)
    context = jnp.einsum(
        "rhl,rlc->rhc", probs, latents[:, :, :LATENT], preferred_element_type=jnp.float32
    )
    return context.astype(jnp.bfloat16)


def wide(value):
    return value.astype(jnp.float32)


def narrow(value):
    return value.astype(jnp.bfloat16)


def gather_whole(value, axis):
    own, below, low, high, above = gather_ring4(value, axis, 0)
    return own, below, jnp.concatenate([low, high], axis=0), above


def halves(value, dim):
    half = value.shape[dim] // 2
    return (
        lax.slice_in_dim(value, 0, half, axis=dim),
        lax.slice_in_dim(value, half, 2 * half, axis=dim),
    )


def gather_ring4(value, axis, half_dim):
    below = shift(value, axis, 1)
    above = shift(value, axis, -1)
    low = shift(halves(below, half_dim)[0], axis, 1)
    high = shift(halves(above, half_dim)[1], axis, -1)
    return value, below, low, high, above


def scatter_ring4(minus, plus, own, below_low, above_high, axis):
    minus = shift(minus, axis, -1)
    plus = shift(plus, axis, 1)
    low = halves(minus, 0)[0]
    high = halves(plus, 0)[1]
    low = shift(narrow(wide(below_low) + wide(low)), axis, -1)
    high = shift(narrow(wide(above_high) + wide(high)), axis, 1)
    return own, minus, plus, low, high


def add_up(own_ref, minus_ref, plus_ref, low_ref, high_ref, start, stop):
    half = own_ref.shape[0] // 2
    if start < half:
        through, ring = plus_ref[start:stop], low_ref[start:stop]
    else:
        through, ring = minus_ref[start:stop], high_ref[start - half : stop - half]
    return narrow(wide(own_ref[start:stop]) + wide(through) + wide(ring))


def relay_kernel(own, minus, plus, low, high, next_minus, next_plus, next_own, below, above):
    mid = TILE // 2
    blocks = [add_up(own, minus, plus, low, high, k * TILE, (k + 1) * TILE) for k in range(4)]
    next_own[...] = blocks[0]
    next_minus[:mid] = blocks[2][:mid]
    next_minus[mid:] = blocks[1][mid:]
    next_plus[:mid] = blocks[3][:mid]
    next_plus[mid:] = blocks[2][mid:]
    below[...] = blocks[1][:mid]
    above[...] = blocks[3][mid:]


def finish_kernel(*refs):
    first, second, out = refs[:5], refs[5:10], refs[10]
    mid = TILE // 2
    half = out.shape[1] // 2
    for side, terms in enumerate((first, second)):
        for start in (0, mid):
            out[start : start + mid, side * half : (side + 1) * half] = add_up(
                *terms, start, start + mid
            )


def product(rows, matrix):
    flat = rows.reshape(-1, rows.shape[-1])
    return jnp.dot(flat, matrix, preferred_element_type=jnp.float32)


TILE = 32
SIDE = 4 * TILE
STEP = 512


def mix(hidden, weight, down_own, down_other, columns):
    units = down_own.shape[0]
    return narrow(
        weight[:, 0:1]
        * jnp.dot(hidden[:, :units], down_own[:, columns], preferred_element_type=jnp.float32)
        + weight[:, 1:2]
        * jnp.dot(hidden[:, units:], down_other[:, columns], preferred_element_type=jnp.float32)
    )


def rows_of(ref, picks):
    return jnp.concatenate([ref[k, start:stop] for k, start, stop in picks], axis=0)


def mix_both(hidden_refs, weight_refs, own_ref, other_ref, out_refs, picks):
    half = own_ref.shape[1] // 2
    for side in (0, 1):
        hidden = rows_of(hidden_refs[side], picks)
        weight = rows_of(weight_refs[side], picks)
        for start in range(0, half, STEP):
            columns = slice(side * half + start, side * half + start + STEP)
            total = mix(hidden, weight, own_ref, other_ref, columns)
            at = 0
            for out_ref in out_refs[side]:
                rows = out_ref.shape[0]
                out_ref[:, start : start + STEP] = total[at : at + rows]
                at += rows


def lead_kernel(*refs):
    first, second, (own_ref, other_ref) = refs[:5], refs[5:10], refs[10:12]
    minus0, plus0, minus1, plus1, h0, h1, w0, w1 = refs[12:]
    pair = h0.shape[-1]

    def tile(blocks, k, place):
        own, below, low, high, above = blocks
        if k == 2:
            ref, place = (low, place) if place < 2 else (high, place - 2)
        else:
            ref = {0: own, 1: below, 3: above}[k]
        return ref[place * TILE : (place + 1) * TILE]

    for x in range(4):
        for y in range(4):
            from_second = tile(second, x, y)
            act = tile(first, y, x) + from_second[:, : 2 * pair]
            weight = from_second[:, 2 * pair :]
            gate = act[:, :pair]
            hidden = narrow(gate / (1.0 + jnp.exp(-gate)) * act[:, pair:])
            h0[y, x * TILE : (x + 1) * TILE] = hidden
            h1[x, y * TILE : (y + 1) * TILE] = hidden
            w0[y, x * TILE : (x + 1) * TILE] = weight
            w1[x, y * TILE : (y + 1) * TILE] = weight
    mid = SIDE // 2
    picks = ((2, 0, mid), (1, mid, SIDE), (3, 0, mid), (2, mid, SIDE))
    outs = ((minus0, plus0), (minus1, plus1))
    mix_both((h0, h1), (w0, w1), own_ref, other_ref, outs, picks)


def rest_kernel(h0, h1, w0, w1, own_ref, other_ref, *outs):
    mid = SIDE // 2
    picks = ((0, 0, SIDE), (1, 0, mid), (3, mid, SIDE))
    mix_both((h0, h1), (w0, w1), own_ref, other_ref, (outs[:3], outs[3:]), picks)


def in_vmem(kernel, args, shapes, flops):
    spec = pl.BlockSpec(memory_space=pltpu.VMEM)
    return pl.pallas_call(
        kernel,
        in_specs=[spec] * len(args),
        out_specs=[spec] * len(shapes),
        out_shape=[jax.ShapeDtypeStruct(shape, dtype) for shape, dtype in shapes],
        compiler_params=pltpu.CompilerParams(vmem_limit_bytes=40 * 1024 * 1024),
        cost_estimate=pl.CostEstimate(flops=flops, bytes_accessed=1 << 20, transcendentals=0),
    )(*args)


def on_device(
    moe_input,
    route_ids,
    route_weight,
    gate_weight,
    up_weight,
    down_weight,
    att_query,
    att_cache,
    cache_length,
):
    rows, width = moe_input.shape
    half = width // 2
    units = gate_weight.shape[2]
    swap = [(0, 1), (1, 0)]
    gate_own, up_own, d_own = gate_weight[0], up_weight[0], down_weight[0]
    gate_other = lax.ppermute(gate_own, "core", swap)
    up_other = lax.ppermute(up_own, "core", swap)
    d_other = lax.ppermute(d_own, "core", swap)

    lanes = lax.broadcasted_iota(jnp.int32, (1, 1, 128), 2)
    routed = route_ids[:, :, None] == lanes
    dense = narrow(jnp.sum(jnp.where(routed, wide(route_weight)[:, :, None], 0.0), axis=1))
    sent = jnp.concatenate([moe_input, dense], axis=1)
    sent = jnp.broadcast_to(sent[None], (8, rows, width + 128))
    sent = lax.all_to_all(sent, "z", 0, 0, tiled=True).reshape(8 * rows, width + 128)
    sent, gate_other, up_other, d_other = lax.optimization_barrier(
        (sent, gate_other, up_other, d_other)
    )
    first = jnp.stack(gather_whole(sent[:, :half], "x"))
    second = jnp.stack(gather_whole(sent[:, half:], "y"))
    first, second, att_query = lax.optimization_barrier((first, second, att_query))
    context = attend(att_query, att_cache, cache_length)
    w_all = jnp.concatenate([gate_own, gate_other, up_own, up_other], axis=1)
    w_first = w_all[:half]
    me = lax.axis_index(("xl", "z", "core"))
    line = lax.broadcasted_iota(jnp.int32, (128, 128), 0)
    lane = lax.broadcasted_iota(jnp.int32, (128, 128), 1)
    chosen = ((lane == 0) & (line == me)) | ((lane == 1) & (line == (me ^ 1)))
    w_second = jnp.pad(w_all[half:], ((0, 128), (0, 128)))
    w_second = lax.dynamic_update_slice(w_second, chosen.astype(jnp.bfloat16), (half, 4 * units))

    first = [product(block, w_first) for block in gather_ring4(first, "y", 0)]
    second = [product(block, w_second) for block in gather_ring4(second, "x", 0)]
    bf16, f32 = jnp.bfloat16, jnp.float32
    whole = ((SIDE, half), bf16)
    part = ((SIDE // 2, half), bf16)
    hidden = ((4, SIDE, 2 * units), bf16)
    weight = ((4, SIDE, 128), f32)
    flops = 2 * 2 * SIDE * 2 * units * width
    minus0, plus0, minus1, plus1, *mids = in_vmem(
        lead_kernel,
        (*first, *second, d_own, d_other),
        [whole] * 4 + [hidden] * 2 + [weight] * 2,
        flops,
    )
    rest = in_vmem(rest_kernel, (*mids, d_own, d_other), [whole, part, part] * 2, flops)

    first = scatter_ring4(minus0, plus0, *rest[:3], "y")
    second = scatter_ring4(minus1, plus1, *rest[3:], "x")
    tile = ((TILE, half), bf16)
    small = ((TILE // 2, half), bf16)
    first = in_vmem(relay_kernel, first, [tile] * 3 + [small] * 2, 1 << 20)
    second = in_vmem(relay_kernel, second, [tile] * 3 + [small] * 2, 1 << 20)
    first = scatter_ring4(*first, "x")
    second = scatter_ring4(*second, "y")
    (mixed,) = in_vmem(finish_kernel, (*first, *second), [((TILE, width), bf16)], 1 << 20)
    mixed = lax.all_to_all(mixed.reshape(8, rows, width), "z", 0, 0, tiled=True)
    return narrow(jnp.sum(wide(mixed), axis=0)), context


def solution(mesh):
    fine = Mesh(mesh.devices.reshape(SIZES), AXES)
    every = AXES
    tp = ("xl", "z", "core")
    dp = ("xh", "y")
    in_specs = (
        P(every, None),
        P(every, None),
        P(every, None),
        P(tp, None, dp),
        P(tp, None, dp),
        P(tp, dp, None),
        P(every, None, None),
        P(every, None, None),
        P(every),
    )
    out_specs = (P(every, None), P(every, None, None))
    return jax.shard_map(
        on_device, mesh=fine, in_specs=in_specs, out_specs=out_specs, check_vma=False
    )
```

```python
import jax
import jax.numpy as jnp
from jax import lax
from jax.experimental import pallas as pl
from jax.experimental.pallas import tpu as pltpu
from jax.sharding import Mesh, PartitionSpec as P

LATENT = 512
AXES = ("xh", "y", "xl", "z", "core")
SIZES = (2, 4, 2, 8, 2)
LENGTH = {"x": 4, "y": 4, "z": 8}
NAMES = {"x": ("xh", "xl"), "y": "y", "z": "z"}
softmax_scale = 192.0 ** (-0.5)


def shift(value, axis, by):
    n = LENGTH[axis]
    return lax.ppermute(value, NAMES[axis], [(i, (i + by) % n) for i in range(n)])


def attend(queries, latents, length):
    scores = (
        jnp.einsum("rhc,rlc->rhl", queries, latents, preferred_element_type=jnp.float32)
        * softmax_scale
    )
    visible = jnp.arange(latents.shape[1], dtype=jnp.int32)[None, None, :] < length[:, None, None]
    scores = jnp.where(visible, scores, -jnp.inf)
    highest = jnp.max(scores, axis=-1, keepdims=True)
    weight = jnp.exp(scores - highest)
    probs = (weight / jnp.sum(weight, axis=-1, keepdims=True)).astype(jnp.bfloat16)
    context = jnp.einsum(
        "rhl,rlc->rhc", probs, latents[:, :, :LATENT], preferred_element_type=jnp.float32
    )
    return context.astype(jnp.bfloat16)


def wide(value):
    return value.astype(jnp.float32)


def narrow(value):
    return value.astype(jnp.bfloat16)


def split_kernel(whole, first, second):
    at = first.shape[1]
    first[...] = whole[:, :at]
    second[...] = whole[:, at:]


def low_kernel(block, out):
    out[...] = block[: out.shape[0]]


def high_kernel(block, out):
    out[...] = block[out.shape[0] :]


def join_kernel(own, below, low, high, above, out):
    half = low.shape[0]
    out[0] = own[...]
    out[1] = below[...]
    out[2, :half] = low[...]
    out[2, half:] = high[...]
    out[3] = above[...]


def gather_whole(own, axis):
    rows, width = own.shape
    part = [((rows // 2, width), own.dtype)]
    below = shift(own, axis, 1)
    above = shift(own, axis, -1)
    (low,) = in_vmem(low_kernel, (below,), part, 1 << 10)
    (high,) = in_vmem(high_kernel, (above,), part, 1 << 10)
    blocks = (own, below, shift(low, axis, 1), shift(high, axis, -1), above)
    return in_vmem(join_kernel, blocks, [((4, rows, width), own.dtype)], 1 << 10)[0]


def halves(value, dim):
    half = value.shape[dim] // 2
    return (
        lax.slice_in_dim(value, 0, half, axis=dim),
        lax.slice_in_dim(value, half, 2 * half, axis=dim),
    )


def gather_ring4(value, axis, half_dim):
    below = shift(value, axis, 1)
    above = shift(value, axis, -1)
    low = shift(halves(below, half_dim)[0], axis, 1)
    high = shift(halves(above, half_dim)[1], axis, -1)
    return value, below, low, high, above


def scatter_ring4(minus, plus, own, below_low, above_high, axis):
    minus = shift(minus, axis, -1)
    plus = shift(plus, axis, 1)
    low = halves(minus, 0)[0]
    high = halves(plus, 0)[1]
    low = shift(narrow(wide(below_low) + wide(low)), axis, -1)
    high = shift(narrow(wide(above_high) + wide(high)), axis, 1)
    return own, minus, plus, low, high


def add_up(own_ref, minus_ref, plus_ref, low_ref, high_ref, start, stop):
    half = own_ref.shape[0] // 2
    if start < half:
        through, ring = plus_ref[start:stop], low_ref[start:stop]
    else:
        through, ring = minus_ref[start:stop], high_ref[start - half : stop - half]
    return narrow(wide(own_ref[start:stop]) + wide(through) + wide(ring))


def relay_kernel(own, minus, plus, low, high, *outs):
    for k, out in enumerate(outs):
        out[...] = add_up(own, minus, plus, low, high, k * TILE, (k + 1) * TILE)


def scatter_direct(parts, axis):
    return (parts[0], *(shift(parts[k], axis, -k) for k in (2, 1, 3)))


def finish_kernel(*refs):
    half = refs[-1].shape[1] // 2
    for side, terms in enumerate((refs[:4], refs[4:8])):
        total = sum(wide(term[...]) for term in terms)
        refs[-1][:, side * half : (side + 1) * half] = narrow(total)


def product(rows, matrix):
    flat = rows.reshape(-1, rows.shape[-1])
    return jnp.dot(flat, matrix, preferred_element_type=jnp.float32)


def start_kernel(rows_ref, ids_ref, weight_ref, out_ref):
    rows, width = rows_ref.shape
    lane = lax.broadcasted_iota(jnp.int32, (rows, 128), 1)
    weight = wide(weight_ref[...])
    dense = jnp.zeros((rows, 128), jnp.float32)
    for k in range(ids_ref.shape[1]):
        dense += jnp.where(lane == ids_ref[:, k : k + 1], weight[:, k : k + 1], 0.0)
    dense = narrow(dense)
    for k in range(out_ref.shape[0]):
        out_ref[k, :, :width] = rows_ref[...]
        out_ref[k, :, width:] = dense


TILE = 32
SIDE = 4 * TILE
STEP = 512


def mix(hidden, weight, down_own, down_other, columns):
    units = down_own.shape[0]
    return narrow(
        weight[:, 0:1]
        * jnp.dot(hidden[:, :units], down_own[:, columns], preferred_element_type=jnp.float32)
        + weight[:, 1:2]
        * jnp.dot(hidden[:, units:], down_other[:, columns], preferred_element_type=jnp.float32)
    )


def rows_of(ref, picks):
    return jnp.concatenate([ref[k, start:stop] for k, start, stop in picks], axis=0)


def mix_both(hidden_refs, weight_refs, own_ref, other_ref, out_refs, picks):
    half = own_ref.shape[1] // 2
    for side in (0, 1):
        hidden = rows_of(hidden_refs[side], picks)
        weight = rows_of(weight_refs[side], picks)
        for start in range(0, half, STEP):
            columns = slice(side * half + start, side * half + start + STEP)
            total = mix(hidden, weight, own_ref, other_ref, columns)
            at = 0
            for out_ref in out_refs[side]:
                rows = out_ref.shape[0]
                out_ref[:, start : start + STEP] = total[at : at + rows]
                at += rows


def lead_kernel(*refs):
    first, second, (own_ref, other_ref) = refs[:5], refs[5:10], refs[10:12]
    minus0, plus0, minus1, plus1, h0, h1, w0, w1 = refs[12:]
    pair = h0.shape[-1]

    def tile(blocks, k, place):
        own, below, low, high, above = blocks
        if k == 2:
            ref, place = (low, place) if place < 2 else (high, place - 2)
        else:
            ref = {0: own, 1: below, 3: above}[k]
        return ref[place * TILE : (place + 1) * TILE]

    for x in range(4):
        for y in range(4):
            from_second = tile(second, x, y)
            act = tile(first, y, x) + from_second[:, : 2 * pair]
            weight = from_second[:, 2 * pair :]
            gate = act[:, :pair]
            hidden = narrow(gate / (1.0 + jnp.exp(-gate)) * act[:, pair:])
            h0[y, x * TILE : (x + 1) * TILE] = hidden
            h1[x, y * TILE : (y + 1) * TILE] = hidden
            w0[y, x * TILE : (x + 1) * TILE] = weight
            w1[x, y * TILE : (y + 1) * TILE] = weight
    mid = SIDE // 2
    picks = ((2, 0, mid), (1, mid, SIDE), (3, 0, mid), (2, mid, SIDE))
    outs = ((minus0, plus0), (minus1, plus1))
    mix_both((h0, h1), (w0, w1), own_ref, other_ref, outs, picks)


def rest_kernel(h0, h1, w0, w1, own_ref, other_ref, *outs):
    mid = SIDE // 2
    picks = ((0, 0, SIDE), (1, 0, mid), (3, mid, SIDE))
    mix_both((h0, h1), (w0, w1), own_ref, other_ref, (outs[:3], outs[3:]), picks)


def in_vmem(kernel, args, shapes, flops):
    spec = pl.BlockSpec(memory_space=pltpu.VMEM)
    return pl.pallas_call(
        kernel,
        in_specs=[spec] * len(args),
        out_specs=[spec] * len(shapes),
        out_shape=[jax.ShapeDtypeStruct(shape, dtype) for shape, dtype in shapes],
        compiler_params=pltpu.CompilerParams(vmem_limit_bytes=8 * 1024 * 1024),
        cost_estimate=pl.CostEstimate(flops=flops, bytes_accessed=1 << 20, transcendentals=0),
    )(*args)


def on_device(
    moe_input,
    route_ids,
    route_weight,
    gate_weight,
    up_weight,
    down_weight,
    att_query,
    att_cache,
    cache_length,
):
    rows, width = moe_input.shape
    half = width // 2
    units = gate_weight.shape[2]
    swap = [(0, 1), (1, 0)]
    gate_own, up_own, d_own = gate_weight[0], up_weight[0], down_weight[0]
    gate_other = lax.ppermute(gate_own, "core", swap)
    up_other = lax.ppermute(up_own, "core", swap)
    d_other = lax.ppermute(d_own, "core", swap)

    bf16, f32 = jnp.bfloat16, jnp.float32
    (sent,) = in_vmem(
        start_kernel,
        (moe_input, route_ids, route_weight),
        [((8, rows, width + 128), bf16)],
        1 << 20,
    )
    sent = lax.all_to_all(sent, "z", 0, 0, tiled=True).reshape(8 * rows, width + 128)
    sent, gate_other, up_other, d_other = lax.optimization_barrier(
        (sent, gate_other, up_other, d_other)
    )
    first, second = in_vmem(
        split_kernel,
        (sent,),
        [((8 * rows, half), bf16), ((8 * rows, half + 128), bf16)],
        1 << 10,
    )
    first = gather_whole(first, "x")
    second = gather_whole(second, "y")
    second, gate_own, up_own, att_query = lax.optimization_barrier(
        (second, gate_own, up_own, att_query)
    )
    context = attend(att_query, att_cache, cache_length)
    w_all = jnp.concatenate([gate_own, gate_other, up_own, up_other], axis=1)
    w_first = w_all[:half]
    me = lax.axis_index(("xl", "z", "core"))
    line = lax.broadcasted_iota(jnp.int32, (128, 128), 0)
    lane = lax.broadcasted_iota(jnp.int32, (128, 128), 1)
    chosen = ((lane == 0) & (line == me)) | ((lane == 1) & (line == (me ^ 1)))
    w_second = jnp.pad(w_all[half:], ((0, 128), (0, 128)))
    w_second = lax.dynamic_update_slice(w_second, chosen.astype(bf16), (half, 4 * units))

    first = [product(block, w_first) for block in gather_ring4(first, "y", 0)]
    second = [product(block, w_second) for block in gather_ring4(second, "x", 0)]
    whole = ((SIDE, half), bf16)
    part = ((SIDE // 2, half), bf16)
    hidden = ((4, SIDE, 2 * units), bf16)
    weight = ((4, SIDE, 128), f32)
    flops = 2 * 2 * SIDE * 2 * units * width
    minus0, plus0, minus1, plus1, *mids = in_vmem(
        lead_kernel,
        (*first, *second, d_own, d_other),
        [whole] * 4 + [hidden] * 2 + [weight] * 2,
        flops,
    )
    rest = in_vmem(rest_kernel, (*mids, d_own, d_other), [whole, part, part] * 2, flops)

    first = scatter_ring4(minus0, plus0, *rest[:3], "y")
    second = scatter_ring4(minus1, plus1, *rest[3:], "x")
    tile = ((TILE, half), bf16)
    first = in_vmem(relay_kernel, first, [tile] * 4, 1 << 20)
    second = in_vmem(relay_kernel, second, [tile] * 4, 1 << 20)
    first = scatter_direct(first, "x")
    second = scatter_direct(second, "y")
    (mixed,) = in_vmem(finish_kernel, (*first, *second), [((TILE, width), bf16)], 1 << 20)
    mixed = lax.all_to_all(mixed.reshape(8, rows, width), "z", 0, 0, tiled=True)
    return narrow(jnp.sum(wide(mixed), axis=0)), context


def solution(mesh):
    fine = Mesh(mesh.devices.reshape(SIZES), AXES)
    every = AXES
    tp = ("xl", "z", "core")
    dp = ("xh", "y")
    in_specs = (
        P(every, None),
        P(every, None),
        P(every, None),
        P(tp, None, dp),
        P(tp, None, dp),
        P(tp, dp, None),
        P(every, None, None),
        P(every, None, None),
        P(every),
    )
    out_specs = (P(every, None), P(every, None, None))
    return jax.shard_map(
        on_device, mesh=fine, in_specs=in_specs, out_specs=out_specs, check_vma=False
    )
```

```python
import jax
import jax.numpy as jnp
from jax import lax
from jax.experimental import pallas as pl
from jax.experimental.pallas import tpu as pltpu
from jax.sharding import Mesh, PartitionSpec as P

LATENT = 512
AXES = ("xh", "y", "xl", "z", "core")
SIZES = (2, 4, 2, 8, 2)
LENGTH = {"x": 4, "y": 4, "z": 8}
NAMES = {"x": ("xh", "xl"), "y": "y", "z": "z"}
softmax_scale = 192.0 ** (-0.5)


def shift(value, axis, by):
    n = LENGTH[axis]
    return lax.ppermute(value, NAMES[axis], [(i, (i + by) % n) for i in range(n)])


def attend(queries, latents, length):
    scores = (
        jnp.einsum("rhc,rlc->rhl", queries, latents, preferred_element_type=jnp.float32)
        * softmax_scale
    )
    visible = jnp.arange(latents.shape[1], dtype=jnp.int32)[None, None, :] < length[:, None, None]
    scores = jnp.where(visible, scores, -jnp.inf)
    highest = jnp.max(scores, axis=-1, keepdims=True)
    weight = jnp.exp(scores - highest)
    probs = (weight / jnp.sum(weight, axis=-1, keepdims=True)).astype(jnp.bfloat16)
    context = jnp.einsum(
        "rhl,rlc->rhc", probs, latents[:, :, :LATENT], preferred_element_type=jnp.float32
    )
    return context.astype(jnp.bfloat16)


def wide(value):
    return value.astype(jnp.float32)


def narrow(value):
    return value.astype(jnp.bfloat16)


def split_kernel(whole, first, second):
    at = first.shape[1]
    first[...] = whole[:, :at]
    second[...] = whole[:, at:]


def stack_kernel(*refs):
    for k, ref in enumerate(refs[:-1]):
        refs[-1][k] = ref[...]


def gather_whole(own, axis):
    below = shift(own, axis, 1)
    above = shift(own, axis, -1)
    blocks = (own, below, shift(below, axis, 1), above)
    shape = (4,) + own.shape
    return in_vmem(stack_kernel, blocks, [(shape, own.dtype)], 1 << 10)[0]


def halves(value, dim):
    half = value.shape[dim] // 2
    return (
        lax.slice_in_dim(value, 0, half, axis=dim),
        lax.slice_in_dim(value, half, 2 * half, axis=dim),
    )


def gather_ring4(value, axis, half_dim):
    below = shift(value, axis, 1)
    above = shift(value, axis, -1)
    low = shift(halves(below, half_dim)[0], axis, 1)
    high = shift(halves(above, half_dim)[1], axis, -1)
    return value, below, low, high, above


def scatter_ring4(minus, plus, own, below_low, above_high, axis):
    minus = shift(minus, axis, -1)
    plus = shift(plus, axis, 1)
    low = halves(minus, 0)[0]
    high = halves(plus, 0)[1]
    low = shift(narrow(wide(below_low) + wide(low)), axis, -1)
    high = shift(narrow(wide(above_high) + wide(high)), axis, 1)
    return own, minus, plus, low, high


def add_up(own_ref, minus_ref, plus_ref, low_ref, high_ref, start, stop):
    half = own_ref.shape[0] // 2
    if start < half:
        through, ring = plus_ref[start:stop], low_ref[start:stop]
    else:
        through, ring = minus_ref[start:stop], high_ref[start - half : stop - half]
    return narrow(wide(own_ref[start:stop]) + wide(through) + wide(ring))


def relay_kernel(own, minus, plus, low, high, *outs):
    for k, out in enumerate(outs):
        out[...] = add_up(own, minus, plus, low, high, k * TILE, (k + 1) * TILE)


def scatter_direct(parts, axis):
    return (parts[0], *(shift(parts[k], axis, -k) for k in (2, 1, 3)))


def finish_kernel(*refs):
    half = refs[-1].shape[1] // 2
    for side, terms in enumerate((refs[:4], refs[4:8])):
        total = sum(wide(term[...]) for term in terms)
        refs[-1][:, side * half : (side + 1) * half] = narrow(total)


def product(rows, matrix):
    flat = rows.reshape(-1, rows.shape[-1])
    return jnp.dot(flat, matrix, preferred_element_type=jnp.float32)


def start_kernel(rows_ref, ids_ref, weight_ref, out_ref):
    rows, width = rows_ref.shape
    lane = lax.broadcasted_iota(jnp.int32, (rows, 128), 1)
    weight = wide(weight_ref[...])
    dense = jnp.zeros((rows, 128), jnp.float32)
    for k in range(ids_ref.shape[1]):
        dense += jnp.where(lane == ids_ref[:, k : k + 1], weight[:, k : k + 1], 0.0)
    dense = narrow(dense)
    for k in range(out_ref.shape[0]):
        out_ref[k, :, :width] = rows_ref[...]
        out_ref[k, :, width:] = dense


TILE = 32
SIDE = 4 * TILE
STEP = 512


def mix(hidden, weight, down_own, down_other, columns):
    units = down_own.shape[0]
    return narrow(
        weight[:, 0:1]
        * jnp.dot(hidden[:, :units], down_own[:, columns], preferred_element_type=jnp.float32)
        + weight[:, 1:2]
        * jnp.dot(hidden[:, units:], down_other[:, columns], preferred_element_type=jnp.float32)
    )


def rows_of(ref, picks):
    return jnp.concatenate([ref[k, start:stop] for k, start, stop in picks], axis=0)


def mix_both(hidden_refs, weight_refs, own_ref, other_ref, out_refs, picks):
    half = own_ref.shape[1] // 2
    for side in (0, 1):
        hidden = rows_of(hidden_refs[side], picks)
        weight = rows_of(weight_refs[side], picks)
        for start in range(0, half, STEP):
            columns = slice(side * half + start, side * half + start + STEP)
            total = mix(hidden, weight, own_ref, other_ref, columns)
            at = 0
            for out_ref in out_refs[side]:
                rows = out_ref.shape[0]
                out_ref[:, start : start + STEP] = total[at : at + rows]
                at += rows


def lead_kernel(*refs):
    first, second, (own_ref, other_ref) = refs[:5], refs[5:10], refs[10:12]
    minus0, plus0, minus1, plus1, h0, h1, w0, w1 = refs[12:]
    pair = h0.shape[-1]

    def tile(blocks, k, place):
        own, below, low, high, above = blocks
        if k == 2:
            ref, place = (low, place) if place < 2 else (high, place - 2)
        else:
            ref = {0: own, 1: below, 3: above}[k]
        return ref[place * TILE : (place + 1) * TILE]

    for x in range(4):
        for y in range(4):
            from_second = tile(second, x, y)
            act = tile(first, y, x) + from_second[:, : 2 * pair]
            weight = from_second[:, 2 * pair :]
            gate = act[:, :pair]
            hidden = narrow(gate / (1.0 + jnp.exp(-gate)) * act[:, pair:])
            h0[y, x * TILE : (x + 1) * TILE] = hidden
            h1[x, y * TILE : (y + 1) * TILE] = hidden
            w0[y, x * TILE : (x + 1) * TILE] = weight
            w1[x, y * TILE : (y + 1) * TILE] = weight
    mid = SIDE // 2
    picks = ((2, 0, mid), (1, mid, SIDE), (3, 0, mid), (2, mid, SIDE))
    outs = ((minus0, plus0), (minus1, plus1))
    mix_both((h0, h1), (w0, w1), own_ref, other_ref, outs, picks)


def rest_kernel(h0, h1, w0, w1, own_ref, other_ref, *outs):
    mid = SIDE // 2
    picks = ((0, 0, SIDE), (1, 0, mid), (3, mid, SIDE))
    mix_both((h0, h1), (w0, w1), own_ref, other_ref, (outs[:3], outs[3:]), picks)


def in_vmem(kernel, args, shapes, flops):
    spec = pl.BlockSpec(memory_space=pltpu.VMEM)
    return pl.pallas_call(
        kernel,
        in_specs=[spec] * len(args),
        out_specs=[spec] * len(shapes),
        out_shape=[jax.ShapeDtypeStruct(shape, dtype) for shape, dtype in shapes],
        compiler_params=pltpu.CompilerParams(vmem_limit_bytes=8 * 1024 * 1024),
        cost_estimate=pl.CostEstimate(flops=flops, bytes_accessed=1 << 20, transcendentals=0),
    )(*args)


def on_device(
    moe_input,
    route_ids,
    route_weight,
    gate_weight,
    up_weight,
    down_weight,
    att_query,
    att_cache,
    cache_length,
):
    rows, width = moe_input.shape
    half = width // 2
    units = gate_weight.shape[2]
    swap = [(0, 1), (1, 0)]
    gate_own, up_own, d_own = gate_weight[0], up_weight[0], down_weight[0]
    gate_other = lax.ppermute(gate_own, "core", swap)
    up_other = lax.ppermute(up_own, "core", swap)
    d_other = lax.ppermute(d_own, "core", swap)

    bf16, f32 = jnp.bfloat16, jnp.float32
    sent = pl.pallas_call(
        start_kernel,
        out_specs=pl.BlockSpec(memory_space=pltpu.VMEM),
        out_shape=jax.ShapeDtypeStruct((8, rows, width + 128), bf16),
        grid=(1,),
        in_specs=[
            pl.BlockSpec(value.shape, lambda i: (0, 0))
            for value in (moe_input, route_ids, route_weight)
        ],
    )(moe_input, route_ids, route_weight)
    sent = lax.all_to_all(sent, "z", 0, 0, tiled=True).reshape(8 * rows, width + 128)
    sent, gate_other, up_other, d_other = lax.optimization_barrier(
        (sent, gate_other, up_other, d_other)
    )
    first, second = in_vmem(
        split_kernel,
        (sent,),
        [((8 * rows, half), bf16), ((8 * rows, half + 128), bf16)],
        1 << 10,
    )
    first = gather_whole(first, "x")
    second = gather_whole(second, "y")
    second, gate_own, up_own, att_query = lax.optimization_barrier(
        (second, gate_own, up_own, att_query)
    )
    context = attend(att_query, att_cache, cache_length)
    w_all = jnp.concatenate([gate_own, gate_other, up_own, up_other], axis=1)
    w_first = w_all[:half]
    me = lax.axis_index(("xl", "z", "core"))
    line = lax.broadcasted_iota(jnp.int32, (128, 128), 0)
    lane = lax.broadcasted_iota(jnp.int32, (128, 128), 1)
    chosen = ((lane == 0) & (line == me)) | ((lane == 1) & (line == (me ^ 1)))
    w_second = jnp.pad(w_all[half:], ((0, 128), (0, 128)))
    w_second = lax.dynamic_update_slice(w_second, chosen.astype(bf16), (half, 4 * units))

    first = [product(block, w_first) for block in gather_ring4(first, "y", 0)]
    second = [product(block, w_second) for block in gather_ring4(second, "x", 0)]
    whole = ((SIDE, half), bf16)
    part = ((SIDE // 2, half), bf16)
    hidden = ((4, SIDE, 2 * units), bf16)
    weight = ((4, SIDE, 128), f32)
    flops = 2 * 2 * SIDE * 2 * units * width
    minus0, plus0, minus1, plus1, *mids = in_vmem(
        lead_kernel,
        (*first, *second, d_own, d_other),
        [whole] * 4 + [hidden] * 2 + [weight] * 2,
        flops,
    )
    rest = in_vmem(rest_kernel, (*mids, d_own, d_other), [whole, part, part] * 2, flops)

    first = scatter_ring4(minus0, plus0, *rest[:3], "y")
    second = scatter_ring4(minus1, plus1, *rest[3:], "x")
    tile = ((TILE, half), bf16)
    first = in_vmem(relay_kernel, first, [tile] * 4, 1 << 20)
    second = in_vmem(relay_kernel, second, [tile] * 4, 1 << 20)
    first = scatter_direct(first, "x")
    second = scatter_direct(second, "y")
    (mixed,) = in_vmem(finish_kernel, (*first, *second), [((TILE, width), bf16)], 1 << 20)
    mixed = lax.all_to_all(mixed.reshape(8, rows, width), "z", 0, 0, tiled=True)
    return narrow(jnp.sum(wide(mixed), axis=0)), context


def solution(mesh):
    fine = Mesh(mesh.devices.reshape(SIZES), AXES)
    every = AXES
    tp = ("xl", "z", "core")
    dp = ("xh", "y")
    in_specs = (
        P(every, None),
        P(every, None),
        P(every, None),
        P(tp, None, dp),
        P(tp, None, dp),
        P(tp, dp, None),
        P(every, None, None),
        P(every, None, None),
        P(every),
    )
    out_specs = (P(every, None), P(every, None, None))
    return jax.shard_map(
        on_device, mesh=fine, in_specs=in_specs, out_specs=out_specs, check_vma=False
    )
```

```python
import jax
import jax.numpy as jnp
from jax import lax
from jax.experimental import pallas as pl
from jax.experimental.pallas import tpu as pltpu
from jax.sharding import Mesh, PartitionSpec as P

LATENT = 512
AXES = ("xh", "y", "xl", "z", "core")
SIZES = (2, 4, 2, 8, 2)
LENGTH = {"x": 4, "y": 4, "z": 8}
NAMES = {"x": ("xh", "xl"), "y": "y", "z": "z"}
softmax_scale = 192.0 ** (-0.5)


def shift(value, axis, by):
    n = LENGTH[axis]
    return lax.ppermute(value, NAMES[axis], [(i, (i + by) % n) for i in range(n)])


def attend(queries, latents, length):
    scores = (
        jnp.einsum("rhc,rlc->rhl", queries, latents, preferred_element_type=jnp.float32)
        * softmax_scale
    )
    visible = jnp.arange(latents.shape[1], dtype=jnp.int32)[None, None, :] < length[:, None, None]
    scores = jnp.where(visible, scores, -jnp.inf)
    highest = jnp.max(scores, axis=-1, keepdims=True)
    weight = jnp.exp(scores - highest)
    probs = (weight / jnp.sum(weight, axis=-1, keepdims=True)).astype(jnp.bfloat16)
    context = jnp.einsum(
        "rhl,rlc->rhc", probs, latents[:, :, :LATENT], preferred_element_type=jnp.float32
    )
    return context.astype(jnp.bfloat16)


def wide(value):
    return value.astype(jnp.float32)


def narrow(value):
    return value.astype(jnp.bfloat16)


def split_kernel(whole, first, second):
    at = first.shape[1]
    first[...] = whole[:, :at]
    second[...] = whole[:, at:]


def stack_kernel(*refs):
    for k, ref in enumerate(refs[:-1]):
        refs[-1][k] = ref[...]


def gather_whole(own, axis):
    below = shift(own, axis, 1)
    above = shift(own, axis, -1)
    blocks = (own, below, shift(below, axis, 1), above)
    shape = (4,) + own.shape
    return in_vmem(stack_kernel, blocks, [(shape, own.dtype)], 1 << 10)[0]


def halves(value, dim):
    half = value.shape[dim] // 2
    return (
        lax.slice_in_dim(value, 0, half, axis=dim),
        lax.slice_in_dim(value, half, 2 * half, axis=dim),
    )


def gather_ring4(value, axis, half_dim):
    below = shift(value, axis, 1)
    above = shift(value, axis, -1)
    low = shift(halves(below, half_dim)[0], axis, 1)
    high = shift(halves(above, half_dim)[1], axis, -1)
    return value, below, low, high, above


def scatter_ring4(minus, plus, own, below_low, above_high, axis):
    minus = shift(minus, axis, -1)
    plus = shift(plus, axis, 1)
    low = halves(minus, 0)[0]
    high = halves(plus, 0)[1]
    low = shift(narrow(wide(below_low) + wide(low)), axis, -1)
    high = shift(narrow(wide(above_high) + wide(high)), axis, 1)
    return own, minus, plus, low, high


def add_up(own_ref, minus_ref, plus_ref, low_ref, high_ref, start, stop):
    half = own_ref.shape[0] // 2
    if start < half:
        through, ring = plus_ref[start:stop], low_ref[start:stop]
    else:
        through, ring = minus_ref[start:stop], high_ref[start - half : stop - half]
    return narrow(wide(own_ref[start:stop]) + wide(through) + wide(ring))


def relay_kernel(own, minus, plus, low, high, *outs):
    for k, out in enumerate(outs):
        out[...] = add_up(own, minus, plus, low, high, k * TILE, (k + 1) * TILE)


def scatter_direct(parts, axis):
    return (parts[0], *(shift(parts[k], axis, -k) for k in (2, 1, 3)))


def finish_kernel(*refs):
    half = refs[-1].shape[1] // 2
    for side, terms in enumerate((refs[:4], refs[4:8])):
        total = sum(wide(term[...]) for term in terms)
        refs[-1][:, side * half : (side + 1) * half] = narrow(total)


def product(rows, matrix):
    flat = rows.reshape(-1, rows.shape[-1])
    return jnp.dot(flat, matrix, preferred_element_type=jnp.float32)


def start_kernel(rows_ref, ids_ref, weight_ref, out_ref):
    rows, width = rows_ref.shape
    lane = lax.broadcasted_iota(jnp.int32, (rows, 128), 1)
    weight = wide(weight_ref[...])
    dense = jnp.zeros((rows, 128), jnp.float32)
    for k in range(ids_ref.shape[1]):
        dense += jnp.where(lane == ids_ref[:, k : k + 1], weight[:, k : k + 1], 0.0)
    dense = narrow(dense)
    for k in range(out_ref.shape[0]):
        out_ref[k, :, :width] = rows_ref[...]
        out_ref[k, :, width:] = dense


TILE = 32
SIDE = 4 * TILE
STEP = 512


def mix(hidden, weight, down_own, down_other, columns):
    units = down_own.shape[0]
    return narrow(
        weight[:, 0:1]
        * jnp.dot(hidden[:, :units], down_own[:, columns], preferred_element_type=jnp.float32)
        + weight[:, 1:2]
        * jnp.dot(hidden[:, units:], down_other[:, columns], preferred_element_type=jnp.float32)
    )


def rows_of(ref, picks):
    return jnp.concatenate([ref[k, start:stop] for k, start, stop in picks], axis=0)


def mix_both(hidden_refs, weight_refs, own_ref, other_ref, out_refs, picks, looped):
    half = own_ref.shape[1] // 2
    for side in (0, 1):
        hidden = rows_of(hidden_refs[side], picks)
        weight = rows_of(weight_refs[side], picks)

        def step(k):
            start = k * STEP
            columns = pl.ds(side * half + start, STEP)
            if looped:
                start = pl.multiple_of(start, STEP)
                columns = pl.ds(pl.multiple_of(side * half + start, STEP), STEP)
            total = mix(hidden, weight, own_ref, other_ref, columns)
            at = 0
            for out_ref in out_refs[side]:
                rows = out_ref.shape[0]
                out_ref[:, pl.ds(start, STEP)] = total[at : at + rows]
                at += rows

        if looped:
            pl.loop(0, half // STEP)(step)
        else:
            for k in range(half // STEP):
                step(k)


def lead_kernel(*refs):
    first, second, (own_ref, other_ref) = refs[:5], refs[5:10], refs[10:12]
    minus0, plus0, minus1, plus1, h0, h1, w0, w1 = refs[12:]
    pair = h0.shape[-1]

    def tile(blocks, k, place):
        own, below, low, high, above = blocks
        if k == 2:
            ref, place = (low, place) if place < 2 else (high, place - 2)
        else:
            ref = {0: own, 1: below, 3: above}[k]
        return ref[place * TILE : (place + 1) * TILE]

    for x in range(4):
        for y in range(4):
            from_second = tile(second, x, y)
            act = tile(first, y, x) + from_second[:, : 2 * pair]
            weight = from_second[:, 2 * pair :]
            gate = act[:, :pair]
            hidden = narrow(gate / (1.0 + jnp.exp(-gate)) * act[:, pair:])
            h0[y, x * TILE : (x + 1) * TILE] = hidden
            h1[x, y * TILE : (y + 1) * TILE] = hidden
            w0[y, x * TILE : (x + 1) * TILE] = weight
            w1[x, y * TILE : (y + 1) * TILE] = weight
    mid = SIDE // 2
    picks = ((2, 0, mid), (1, mid, SIDE), (3, 0, mid), (2, mid, SIDE))
    outs = ((minus0, plus0), (minus1, plus1))
    mix_both((h0, h1), (w0, w1), own_ref, other_ref, outs, picks, False)


def rest_kernel(h0, h1, w0, w1, own_ref, other_ref, *outs):
    mid = SIDE // 2
    picks = ((0, 0, SIDE), (1, 0, mid), (3, mid, SIDE))
    mix_both((h0, h1), (w0, w1), own_ref, other_ref, (outs[:3], outs[3:]), picks, True)


def in_vmem(kernel, args, shapes, flops):
    spec = pl.BlockSpec(memory_space=pltpu.VMEM)
    return pl.pallas_call(
        kernel,
        in_specs=[spec] * len(args),
        out_specs=[spec] * len(shapes),
        out_shape=[jax.ShapeDtypeStruct(shape, dtype) for shape, dtype in shapes],
        compiler_params=pltpu.CompilerParams(vmem_limit_bytes=8 * 1024 * 1024),
        cost_estimate=pl.CostEstimate(flops=flops, bytes_accessed=1 << 20, transcendentals=0),
    )(*args)


def on_device(
    moe_input,
    route_ids,
    route_weight,
    gate_weight,
    up_weight,
    down_weight,
    att_query,
    att_cache,
    cache_length,
):
    rows, width = moe_input.shape
    half = width // 2
    units = gate_weight.shape[2]
    swap = [(0, 1), (1, 0)]
    gate_own, up_own, d_own = gate_weight[0], up_weight[0], down_weight[0]
    gate_other = lax.ppermute(gate_own, "core", swap)
    up_other = lax.ppermute(up_own, "core", swap)
    d_other = lax.ppermute(d_own, "core", swap)

    bf16, f32 = jnp.bfloat16, jnp.float32
    sent = pl.pallas_call(
        start_kernel,
        out_specs=pl.BlockSpec(memory_space=pltpu.VMEM),
        out_shape=jax.ShapeDtypeStruct((8, rows, width + 128), bf16),
        grid=(1,),
        in_specs=[
            pl.BlockSpec(value.shape, lambda i: (0, 0))
            for value in (moe_input, route_ids, route_weight)
        ],
    )(moe_input, route_ids, route_weight)
    sent = lax.all_to_all(sent, "z", 0, 0, tiled=True).reshape(8 * rows, width + 128)
    sent, gate_other, up_other, d_other = lax.optimization_barrier(
        (sent, gate_other, up_other, d_other)
    )
    first, second = in_vmem(
        split_kernel,
        (sent,),
        [((8 * rows, half), bf16), ((8 * rows, half + 128), bf16)],
        1 << 10,
    )
    first = gather_whole(first, "x")
    second = gather_whole(second, "y")
    second, gate_own, up_own, att_query = lax.optimization_barrier(
        (second, gate_own, up_own, att_query)
    )
    context = attend(att_query, att_cache, cache_length)
    w_all = jnp.concatenate([gate_own, gate_other, up_own, up_other], axis=1)
    w_first = w_all[:half]
    me = lax.axis_index(("xl", "z", "core"))
    line = lax.broadcasted_iota(jnp.int32, (128, 128), 0)
    lane = lax.broadcasted_iota(jnp.int32, (128, 128), 1)
    chosen = ((lane == 0) & (line == me)) | ((lane == 1) & (line == (me ^ 1)))
    w_second = jnp.pad(w_all[half:], ((0, 128), (0, 128)))
    w_second = lax.dynamic_update_slice(w_second, chosen.astype(bf16), (half, 4 * units))

    first = [product(block, w_first) for block in gather_ring4(first, "y", 0)]
    second = [product(block, w_second) for block in gather_ring4(second, "x", 0)]
    whole = ((SIDE, half), bf16)
    part = ((SIDE // 2, half), bf16)
    hidden = ((4, SIDE, 2 * units), bf16)
    weight = ((4, SIDE, 128), f32)
    flops = 2 * 2 * SIDE * 2 * units * width
    minus0, plus0, minus1, plus1, *mids = in_vmem(
        lead_kernel,
        (*first, *second, d_own, d_other),
        [whole] * 4 + [hidden] * 2 + [weight] * 2,
        flops,
    )
    rest = in_vmem(rest_kernel, (*mids, d_own, d_other), [whole, part, part] * 2, flops)

    first = scatter_ring4(minus0, plus0, *rest[:3], "y")
    second = scatter_ring4(minus1, plus1, *rest[3:], "x")
    tile = ((TILE, half), bf16)
    first = in_vmem(relay_kernel, first, [tile] * 4, 1 << 20)
    second = in_vmem(relay_kernel, second, [tile] * 4, 1 << 20)
    first = scatter_direct(first, "x")
    second = scatter_direct(second, "y")
    (mixed,) = in_vmem(finish_kernel, (*first, *second), [((TILE, width), bf16)], 1 << 20)
    mixed = lax.all_to_all(mixed.reshape(8, rows, width), "z", 0, 0, tiled=True)
    return narrow(jnp.sum(wide(mixed), axis=0)), context


def solution(mesh):
    fine = Mesh(mesh.devices.reshape(SIZES), AXES)
    every = AXES
    tp = ("xl", "z", "core")
    dp = ("xh", "y")
    in_specs = (
        P(every, None),
        P(every, None),
        P(every, None),
        P(tp, None, dp),
        P(tp, None, dp),
        P(tp, dp, None),
        P(every, None, None),
        P(every, None, None),
        P(every),
    )
    out_specs = (P(every, None), P(every, None, None))
    return jax.shard_map(
        on_device, mesh=fine, in_specs=in_specs, out_specs=out_specs, check_vma=False
    )
```
